32 devices in a mesh: blk: 8 (over y, x, core), orb: 4 (over z).
Axes of the slice: x: 2, y: 2, z: 4, core: 2. Of those that a mesh axis runs over, the one named last changes fastest.
Arguments:
- green_tiles: bfloat16 [2, 192, 256, 256], P(None, 'blk'), may hold values from -6 to 6
- screen_tiles: bfloat16 [2, 96, 256, 256], P(None, 'blk', 'orb'), may hold values from -6 to 6
- coeffs: bfloat16 [12288, 2048], P('blk', 'orb'), may hold values from -0.099609375 to 0.099609375
- tile_count: int32 [8], P('blk'), may hold values from 1 to 24, 96 in all
- send_slot: int32 [8, 8, 3], P('blk'), may hold values from 0 to 11
- recv_index: int32 [8, 24], P('blk'), may hold values from 0 to 23, as said below
- row_block: int32 [8, 24], P('blk'), may hold values from 0 to 5
- col_block: int32 [8, 24], P('blk'), may hold values from 0 to 47
Outputs:
- sigma_orbital: float32 [2048, 2, 2048], P('blk', None, 'orb')
The draws below stay inside these ranges and needn't reach their ends.
Inputs may be any that keep to these rules, and one draw needn't show every extreme that they name: `recv_index`: for each blk index and each round r < 3, the slots r * (8) to (r + 1) * 8 - 1 name every peer once, each as peer * 3 + r. `tile_count`: the counts of all blk indices sum to 96.
All inputs are finite; a program needn't handle non-finite values. No bound on the sum of `tile_count` on one device may be relied on, other than what follows from the above.
Results may differ from the reference program's by a relative error of at most 0.0041.
Values may be sent and summed in bfloat16 or wider, within the bound.
A program may use at most 128 MiB of HBM per device.

```python
import math
import jax
import jax.numpy as jnp
import numpy as np
from jax import lax

TILE = 256
NORB = 2048
BLK_DEV = 6
CAP = 3
SLOTS = 24
WSLOTS = 12
NB = 48
NBAS = 12288
N_BLK = 8


def draw_recv_index(key, part):
    peers = SLOTS // CAP
    keys = jax.random.split(key, peers * CAP)
    orders = jax.vmap(lambda single: jax.random.permutation(single, peers))(keys)
    orders = orders.astype(jnp.int32).reshape(peers, CAP, peers)
    rounds = jnp.arange(CAP, dtype=jnp.int32)[None, :, None]
    return (orders * CAP + rounds).reshape(peers, CAP * peers)


def place_ends(entries, stream_key, least, top_value):
    spot = [jax.random.randint(jax.random.fold_in(stream_key, axis), (), 0, length) for axis, length in enumerate(entries.shape)]
    main_axis = entries.shape.index(max(entries.shape))
    next_to = spot[:main_axis] + [(spot[main_axis] + 1) % entries.shape[main_axis]] + spot[main_axis + 1:]
    return entries.at[tuple(spot)].set(least).at[tuple(next_to)].set(top_value)


def raised(drawn, own_key, source, target, shards_of, factor):
    owner, partner = [(jnp.arange(drawn.shape[dim]) // (drawn.shape[dim] // shards_of)).reshape([-1 if axis == dim else 1 for axis in range(drawn.ndim)]) for dim in (source, target)]
    chosen = jax.random.permutation(own_key, shards_of)[partner]
    strong = (owner == chosen) | (owner == (partner + shards_of // 2) % shards_of)
    return jnp.where(strong, factor * drawn, drawn)


def level_of(stream_key, dims, cuts, least, high):
    gain = 1.0
    for dim, shards_of in cuts:
        draws = jax.random.uniform(jax.random.fold_in(jax.random.fold_in(stream_key, 6), dim), (shards_of,), jnp.float32, least / len(cuts), high / len(cuts))
        gain = gain * jnp.repeat(jnp.exp(draws), dims[dim] // shards_of).reshape((-1,) + (1,) * (len(dims) - 1 - dim))
    return gain


def profile(amount, total, limit, skew):
    weights = [(1 << 20) // math.isqrt(standing ** skew) + 1 for standing in range(2, amount + 1)]
    rest, counts = total - limit - (amount - 1), [1] * (amount - 1)
    while rest > 0:
        free = [i for i in range(amount - 1) if counts[i] < limit]
        whole, budget = sum([weights[i] for i in free]), rest
        for i in free:
            more = min(limit - counts[i], max(1, budget * weights[i] // whole), rest)
            counts[i] = counts[i] + more
            rest = rest - more
    return np.array([limit] + counts)


def uneven_parts(rng, number_of, total, reach, lean):
    if number_of == 2:
        one = jax.random.randint(rng, (), max(1, total - reach), min(reach, total - 1) + 1)
        return jnp.stack([one, total - one])
    lengths = jnp.asarray(profile(number_of, total, reach, lean), jnp.int32)
    pairs = (number_of - 1) // 2
    giver, sink = lengths[1:1 + 2 * pairs:2], lengths[2:2 + 2 * pairs:2]
    slack = jnp.minimum(giver - 1, reach - sink)
    shifted = jax.random.randint(jax.random.fold_in(rng, 1), (pairs,), 0, 1 << 20) % (slack + 1)
    lengths = lengths.at[1:1 + 2 * pairs:2].set(giver - shifted).at[2:2 + 2 * pairs:2].set(sink + shifted)
    return lengths[jax.random.permutation(jax.random.fold_in(rng, 2), number_of)]


def noise(stream_key, dims, spread, most, cuts=(), kind=jnp.bfloat16):
    result = spread * jax.random.normal(stream_key, dims, jnp.float32)
    if cuts:
        result = result * level_of(stream_key, dims, cuts, -0.22, 0.18)
    return jnp.clip(result, -most, most).astype(kind)


def heavy_noise(rng, extent, scale, reach, pieces, heavy, kind=jnp.bfloat16):
    drawn = scale * jax.random.normal(rng, extent, jnp.float32)
    if pieces:
        drawn = drawn * level_of(rng, extent, pieces, -0.22, 0.18)
    return jnp.clip(raised(drawn, jax.random.fold_in(rng, 3), *heavy), -reach, reach).astype(kind)


def setup_inputs(seed: int = 0) -> dict:
    key_list = jax.random.split(jax.random.key(seed), 9)
    green_tiles = noise(key_list[0], (2, N_BLK * SLOTS, TILE, TILE), 1.0, 6.0, ((1, 8),))
    screen_tiles = noise(key_list[1], (2, N_BLK * WSLOTS, TILE, TILE), 1.0, 6.0, ((1, 8), (2, 4)))
    coeffs = heavy_noise(key_list[2], (NBAS, NORB), 0.0156, 0.099609375, ((0, 8), (1, 4)), (0, 1, 8, 2.0))
    tile_count = uneven_parts(key_list[3], N_BLK, N_BLK * SLOTS // 2, SLOTS, 2).astype(jnp.int32)
    send_slot = place_ends(jax.random.randint(key_list[4], (N_BLK, N_BLK, CAP), 0, WSLOTS), jax.random.fold_in(key_list[4], 1), 0, WSLOTS - 1).astype(jnp.int32)
    recv_index = draw_recv_index(jax.random.fold_in(key_list[8], 71), 0)
    row_block = place_ends(jax.random.randint(key_list[6], (N_BLK, SLOTS), 0, BLK_DEV), jax.random.fold_in(key_list[6], 1), 0, BLK_DEV - 1).astype(jnp.int32)
    col_block = place_ends(jax.random.randint(key_list[7], (N_BLK, SLOTS), 0, NB), jax.random.fold_in(key_list[7], 1), 0, NB - 1).astype(jnp.int32)
    return dict(green_tiles=green_tiles, screen_tiles=screen_tiles, coeffs=coeffs, tile_count=tile_count, send_slot=send_slot, recv_index=recv_index, row_block=row_block, col_block=col_block)


def reference(green_tiles, screen_tiles, coeffs, tile_count, send_slot, recv_index, row_block, col_block):
    width = green_tiles.shape[2]
    slot_total = recv_index.shape[1]
    blk_count = recv_index.shape[0]
    sends = send_slot.shape[2]
    stock = screen_tiles.shape[1] // blk_count
    owned_blocks = coeffs.shape[0] // (width * blk_count)
    orbitals = coeffs.shape[1]

    def one_device(total, device):
        def one_slot(accum, slot):
            code = recv_index[device, slot]
            source = code // sends
            position = code % sends
            held = send_slot[source, device, position]
            screen = lax.dynamic_index_in_dim(screen_tiles, (source * stock + held).astype(jnp.int32), 1, keepdims=False)
            green = lax.dynamic_index_in_dim(green_tiles, (device * slot_total + slot).astype(jnp.int32), 1, keepdims=False)
            sigma = (-(green.astype(jnp.float32) * screen.astype(jnp.float32))).astype(jnp.bfloat16)
            block = lax.dynamic_slice_in_dim(coeffs, (col_block[device, slot] * width).astype(jnp.int32), width, 0)
            product = jnp.einsum("tab,bm->atm", sigma.astype(jnp.float32), block.astype(jnp.float32))
            live = (slot < tile_count[device]).astype(jnp.float32)
            pick = (jnp.arange(owned_blocks, dtype=jnp.int32) == row_block[device, slot]).astype(jnp.float32) * live
            return accum + pick[:, None, None, None] * product[None], None

        start_acc = jnp.zeros((owned_blocks, width, 2, orbitals), jnp.float32)
        accum, unused = lax.scan(one_slot, start_acc, jnp.arange(slot_total, dtype=jnp.int32))
        folded = accum.astype(jnp.bfloat16).reshape(owned_blocks * width, 2, orbitals)
        own_rows = lax.dynamic_slice_in_dim(coeffs, (device * owned_blocks * width).astype(jnp.int32), owned_blocks * width, 0)
        total = total + jnp.einsum("kn,ktm->ntm", own_rows.astype(jnp.float32), folded.astype(jnp.float32))
        return total, None

    start_total = jnp.zeros((orbitals, 2, orbitals), jnp.float32)
    total, unused = lax.scan(one_device, start_total, jnp.arange(blk_count, dtype=jnp.int32))
    return total
```

```python
import functools

import jax
import jax.numpy as jnp
from jax import lax
from jax.experimental import pallas as pl
from jax.experimental.pallas import tpu as pltpu
from jax.sharding import PartitionSpec as P

MESH = pl.DeviceIdType.MESH
ANY = pl.BlockSpec(memory_space=pl.ANY)


def flip(index, mask):
    bit = 1
    while bit <= mask:
        if mask & bit:
            index = index + bit * (1 - 2 * lax.rem(lax.div(index, bit), 2))
        bit *= 2
    return index


def remote(src, dst, send, recv, blk, orb):
    return pltpu.make_async_remote_copy(
        src_ref=src, dst_ref=dst, send_sem=send, recv_sem=recv,
        device_id=(blk, orb), device_id_type=MESH,
    )


def greet(barrier, blk, orb):
    pl.semaphore_signal(barrier, inc=1, device_id=(blk, orb), device_id_type=MESH)


def gather_kernel(n_blk, n_orb, screen, coeffs, whole, panel, local, zsend, zrecv,
                  psend, precv, fsend, frecv):
    me, z = lax.axis_index("blk"), lax.axis_index("orb")
    partner = flip(me, 1)
    masks = list(range(2, n_blk, 2))
    barrier = pltpu.get_barrier_semaphore()

    @pl.when(z > 0)
    def _():
        greet(barrier, me, z - 1)

    @pl.when(z < n_orb - 1)
    def _():
        greet(barrier, me, z + 1)

    for mask in [1] + masks:
        greet(barrier, flip(me, mask), z)
    pl.semaphore_wait(barrier, len(masks) + 1 + jnp.minimum(z, 1) + jnp.minimum(n_orb - 1 - z, 1))

    def down(src, block):
        return remote(block, whole.at[src], zsend.at[0, src], zrecv.at[src], me, z - 1)

    def up(src, block):
        return remote(block, whole.at[src], zsend.at[1, src], zrecv.at[src], me, z + 1)

    @pl.when(z > 0)
    def _():
        down(z, screen).start()

    @pl.when(z < n_orb - 1)
    def _():
        up(z, screen).start()

    def direct(mask):
        return remote(coeffs, panel.at[me], psend.at[mask // 2], precv.at[mask // 2], flip(me, mask), z)

    for mask in masks:
        direct(mask).start()

    def forward(mask):
        owner = flip(me, mask)
        block = coeffs if mask == 0 else panel.at[owner]
        return remote(block, panel.at[owner], fsend.at[mask // 2], frecv.at[mask // 2], partner, z)

    forward(0).start()
    own_screen = pltpu.make_async_copy(screen, whole.at[z], local.at[0])
    own_coeffs = pltpu.make_async_copy(coeffs, panel.at[me], local.at[1])
    own_screen.start()
    own_coeffs.start()

    for step in range(1, max(n_orb, len(masks) + 1)):
        if step < n_orb:
            @pl.when(z - step >= 0)
            def _():
                src = z - step
                up(src, whole.at[src]).wait_recv()

                @pl.when(z < n_orb - 1)
                def _():
                    up(src, whole.at[src]).start()

            @pl.when(z + step < n_orb)
            def _():
                src = z + step
                down(src, whole.at[src]).wait_recv()

                @pl.when(z > 0)
                def _():
                    down(src, whole.at[src]).start()
        if step - 1 < len(masks):
            mask = masks[step - 1]
            owner = flip(me, mask)
            remote(coeffs, panel.at[owner], psend.at[mask // 2], precv.at[mask // 2], owner, z).wait_recv()
            forward(mask).start()

    own_screen.wait()
    own_coeffs.wait()
    for mask in masks:
        direct(mask).wait_send()
    for mask in [0] + masks:
        forward(mask).wait_send()
        owner = flip(partner, mask)
        remote(coeffs, panel.at[owner], fsend.at[mask // 2], frecv.at[mask // 2], partner, z).wait_recv()

    for src in range(n_orb):
        @pl.when((z > 0) & (src >= z))
        def _():
            down(src, whole.at[src]).wait_send()

        @pl.when((z < n_orb - 1) & (src <= z))
        def _():
            up(src, whole.at[src]).wait_send()


def gather(screen, coeffs, n_blk, n_orb):
    dma = pltpu.SemaphoreType.DMA
    return pl.pallas_call(
        functools.partial(gather_kernel, n_blk, n_orb),
        out_shape=(
            jax.ShapeDtypeStruct((n_orb,) + screen.shape, screen.dtype),
            jax.ShapeDtypeStruct((n_blk,) + coeffs.shape, coeffs.dtype),
        ),
        in_specs=[ANY, ANY],
        out_specs=(ANY, ANY),
        scratch_shapes=[
            dma((2,)), dma((2, n_orb)), dma((n_orb,)),
            dma((n_blk // 2,)), dma((n_blk // 2,)), dma((n_blk // 2,)), dma((n_blk // 2,)),
        ],
        compiler_params=pltpu.CompilerParams(collective_id=1, has_side_effects=True),
        name="gather",
    )(screen, coeffs)


def pack(whole, outgoing):
    n_orb, times, _, rows, width = whole.shape
    total = outgoing.shape[0]

    def body(slots, tile, out):
        for q in range(n_orb):
            out[0, :, q * rows:(q + 1) * rows, :] = tile[q, :, 0]

    return pl.pallas_call(
        body,
        out_shape=jax.ShapeDtypeStruct((total, times, n_orb * rows, width), whole.dtype),
        grid_spec=pltpu.PrefetchScalarGridSpec(
            num_scalar_prefetch=1,
            grid=(total,),
            in_specs=[pl.BlockSpec((n_orb, times, 1, rows, width), lambda j, slots: (0, 0, slots[j], 0, 0))],
            out_specs=pl.BlockSpec((1, times, n_orb * rows, width), lambda j, slots: (j, 0, 0, 0)),
        ),
        name="pack",
    )(outgoing, whole)


def exchange_kernel(n_blk, packed, arrived, local, send, recv):
    me, z = lax.axis_index("blk"), lax.axis_index("orb")
    barrier = pltpu.get_barrier_semaphore()
    for mask in range(1, n_blk):
        greet(barrier, flip(me, mask), z)
    pl.semaphore_wait(barrier, n_blk - 1)

    def copy(mask):
        peer = flip(me, mask)
        return remote(packed.at[peer], arrived.at[me], send.at[mask], recv.at[mask], peer, z)

    order = sorted(range(1, n_blk), key=lambda mask: -bin(mask).count("1"))
    for mask in order:
        copy(mask).start()
    own = pltpu.make_async_copy(packed.at[me], arrived.at[me], local)
    own.start()
    own.wait()
    for mask in order:
        copy(mask).wait_send()
        peer = flip(me, mask)
        remote(packed.at[peer], arrived.at[peer], send.at[mask], recv.at[mask], peer, z).wait_recv()


def exchange(packed, n_blk):
    dma = pltpu.SemaphoreType.DMA
    return pl.pallas_call(
        functools.partial(exchange_kernel, n_blk),
        out_shape=jax.ShapeDtypeStruct(packed.shape, packed.dtype),
        in_specs=[ANY],
        out_specs=ANY,
        scratch_shapes=[dma, dma((n_blk,)), dma((n_blk,))],
        compiler_params=pltpu.CompilerParams(collective_id=2, has_side_effects=True),
        name="exchange",
    )(packed)


def rows_kernel(count, codes, targets, columns, green, screen, block, out, acc):
    slot = pl.program_id(0)
    orbitals = block.shape[2]

    @pl.when(slot == 0)
    def _():
        acc[...] = jnp.zeros_like(acc)

    @pl.when(slot < count[0])
    def _():
        target = targets[slot]
        for t in range(green.shape[0]):
            sigma = (-(green[t, 0].astype(jnp.float32) * screen[0, t].astype(jnp.float32))).astype(jnp.bfloat16)
            acc[target, :, t * orbitals:(t + 1) * orbitals] += jnp.dot(
                sigma, block[0], preferred_element_type=jnp.float32
            )

    @pl.when(slot == pl.num_programs(0) - 1)
    def _():
        for i in range(acc.shape[0]):
            out[i] = acc[i].astype(out.dtype)


def row_sums(green, arrived, blocks, count, codes, targets, columns, owned):
    times, slots, width, _ = green.shape
    orbitals = blocks.shape[2]

    def live(s, count):
        return jnp.minimum(s, count[0] - 1)

    return pl.pallas_call(
        rows_kernel,
        out_shape=jax.ShapeDtypeStruct((owned, width, times * orbitals), jnp.bfloat16),
        grid_spec=pltpu.PrefetchScalarGridSpec(
            num_scalar_prefetch=4,
            grid=(slots,),
            in_specs=[
                pl.BlockSpec((times, 1, width, width), lambda s, n, c, r, k: (0, live(s, n), 0, 0)),
                pl.BlockSpec((1, times, width, width), lambda s, n, c, r, k: (c[live(s, n)], 0, 0, 0)),
                pl.BlockSpec((1, width, orbitals), lambda s, n, c, r, k: (k[live(s, n)], 0, 0)),
            ],
            out_specs=pl.BlockSpec((owned, width, times * orbitals), lambda s, n, c, r, k: (0, 0, 0)),
            scratch_shapes=[pltpu.VMEM((owned, width, times * orbitals), jnp.float32)],
        ),
        compiler_params=pltpu.CompilerParams(vmem_limit_bytes=56 * 2**20),
        name="row_sums",
    )(count, codes, targets, columns, green, arrived, blocks)


def scatter_kernel(n_blk, part, out, first, second, stage, total, ssend, srecv, send, recv):
    me, z = lax.axis_index("blk"), lax.axis_index("orb")
    partner = flip(me, 1)
    masks = sorted(range(2, n_blk, 2), key=lambda mask: -bin(mask).count("1"))
    barrier = pltpu.get_barrier_semaphore()
    for mask in [1] + masks:
        greet(barrier, flip(me, mask), z)
    pl.semaphore_wait(barrier, len(masks) + 1)

    def to_partner(mask):
        h = mask // 2
        return remote(part.at[flip(partner, mask)], first.at[h], ssend.at[h], srecv.at[h], partner, z)

    def to_owner(mask):
        h = mask // 2
        return remote(stage.at[h], second.at[h], send.at[h], recv.at[h], flip(me, mask), z)

    for mask in masks + [0]:
        to_partner(mask).start()
    for mask in masks:
        h = mask // 2
        to_partner(mask).wait_recv()
        stage[h] = (part[flip(me, mask)].astype(jnp.float32) + first[h].astype(jnp.float32)).astype(stage.dtype)
        to_owner(mask).start()
    to_partner(0).wait_recv()
    total[...] = part[me].astype(jnp.float32) + first[0].astype(jnp.float32)
    for mask in masks[::-1]:
        to_owner(mask).wait_recv()
        total[...] += second[mask // 2].astype(jnp.float32)
    out[...] = total[...]
    for mask in masks + [0]:
        to_partner(mask).wait_send()
    for mask in masks:
        to_owner(mask).wait_send()


def scatter(part):
    n_blk, rows, columns = part.shape
    half = n_blk // 2
    dma = pltpu.SemaphoreType.DMA
    vmem = pl.BlockSpec(memory_space=pltpu.VMEM)
    return pl.pallas_call(
        functools.partial(scatter_kernel, n_blk),
        out_shape=jax.ShapeDtypeStruct((rows, columns), jnp.float32),
        in_specs=[vmem],
        out_specs=vmem,
        scratch_shapes=[
            pltpu.VMEM((half, rows, columns), jnp.bfloat16),
            pltpu.VMEM((half, rows, columns), jnp.bfloat16),
            pltpu.VMEM((half, rows, columns), jnp.bfloat16),
            pltpu.VMEM((rows, columns), jnp.float32),
            dma((half,)), dma((half,)), dma((half,)), dma((half,)),
        ],
        compiler_params=pltpu.CompilerParams(
            collective_id=3, has_side_effects=True, vmem_limit_bytes=32 * 2**20
        ),
        name="scatter",
    )(part)


def shards(
    n_blk, n_orb, green_tiles, screen_tiles, coeffs, tile_count, send_slot, recv_index, row_block, col_block
):
    times, _, width, _ = green_tiles.shape
    owned = coeffs.shape[0] // width
    orbitals = coeffs.shape[1]
    whole, panel = gather(screen_tiles, coeffs, n_blk, n_orb)
    own_rows = lax.all_gather(coeffs, "orb", axis=0)
    packed = pack(whole, send_slot.reshape(-1))
    arrived = exchange(packed.reshape((n_blk, -1) + packed.shape[1:]), n_blk)
    folded = row_sums(
        green_tiles, arrived.reshape(packed.shape), panel.reshape(-1, width, orbitals),
        tile_count, recv_index[0], row_block[0], col_block[0], owned,
    ).reshape(owned * width, times * orbitals)
    part = jnp.einsum("zkn,km->znm", own_rows, folded, preferred_element_type=jnp.float32)
    part = part.astype(jnp.bfloat16).reshape(n_blk, -1, times * orbitals)
    return scatter(part).reshape(-1, times, orbitals)


def solution(mesh):
    return jax.shard_map(
        functools.partial(shards, mesh.shape["blk"], mesh.shape["orb"]),
        mesh=mesh,
        in_specs=(
            P(None, "blk", None, None),
            P(None, "blk", "orb", None),
            P("blk", "orb"),
            P("blk"),
            P("blk", None, None),
            P("blk", None),
            P("blk", None),
            P("blk", None),
        ),
        out_specs=P("blk", None, "orb"),
        check_vma=False,
    )
```

```python
import functools

import jax
import jax.numpy as jnp
from jax import lax
from jax.experimental import pallas as pl
from jax.experimental.pallas import tpu as pltpu
from jax.sharding import PartitionSpec as P

MESH = pl.DeviceIdType.MESH
ANY = pl.BlockSpec(memory_space=pl.ANY)


def flip(index, mask):
    bit = 1
    while bit <= mask:
        if mask & bit:
            index = index + bit * (1 - 2 * lax.rem(lax.div(index, bit), 2))
        bit *= 2
    return index


def remote(src, dst, send, recv, blk, orb):
    return pltpu.make_async_remote_copy(
        src_ref=src, dst_ref=dst, send_sem=send, recv_sem=recv,
        device_id=(blk, orb), device_id_type=MESH,
    )


def greet(barrier, blk, orb):
    pl.semaphore_signal(barrier, inc=1, device_id=(blk, orb), device_id_type=MESH)


def line_peers(z, n_orb):
    return jnp.minimum(z, 1) + jnp.minimum(n_orb - 1 - z, 1)


class Line:
    def __init__(self, n_orb, me, z, own, held, send, recv):
        self.n_orb, self.me, self.z, self.own = n_orb, me, z, own
        self.held, self.send, self.recv = held, send, recv

    def down(self, src, block=None):
        block = self.held.at[src] if block is None else block
        return remote(block, self.held.at[src], self.send.at[0, src], self.recv.at[src], self.me, self.z - 1)

    def up(self, src, block=None):
        block = self.held.at[src] if block is None else block
        return remote(block, self.held.at[src], self.send.at[1, src], self.recv.at[src], self.me, self.z + 1)

    def start(self):
        @pl.when(self.z > 0)
        def _():
            self.down(self.z, self.own).start()

        @pl.when(self.z < self.n_orb - 1)
        def _():
            self.up(self.z, self.own).start()

    def step(self, distance):
        @pl.when(self.z - distance >= 0)
        def _():
            src = self.z - distance
            self.up(src).wait_recv()

            @pl.when(self.z < self.n_orb - 1)
            def _():
                self.up(src).start()

        @pl.when(self.z + distance < self.n_orb)
        def _():
            src = self.z + distance
            self.down(src).wait_recv()

            @pl.when(self.z > 0)
            def _():
                self.down(src).start()

    def sent(self):
        for src in range(self.n_orb):
            @pl.when((self.z > 0) & (src >= self.z))
            def _():
                self.down(src).wait_send()

            @pl.when((self.z < self.n_orb - 1) & (src <= self.z))
            def _():
                self.up(src).wait_send()


def spread_kernel(n_blk, n_orb, cap, slots, screen, coeffs, arrived, panel, rows, whole, packed, local, zsend,
                  zrecv, csend, crecv, psend, precv, fsend, frecv, xsend, xrecv):
    me, z = lax.axis_index("blk"), lax.axis_index("orb")
    partner = flip(me, 1)
    masks = list(range(2, n_blk, 2))
    order = sorted(range(1, n_blk), key=lambda mask: -bin(mask).count("1"))
    height = screen.shape[2]
    barrier = pltpu.get_barrier_semaphore()

    @pl.when(z > 0)
    def _():
        greet(barrier, me, z - 1)

    @pl.when(z < n_orb - 1)
    def _():
        greet(barrier, me, z + 1)

    for mask in range(1, n_blk):
        greet(barrier, flip(me, mask), z)
    pl.semaphore_wait(barrier, n_blk - 1 + line_peers(z, n_orb))

    tiles = Line(n_orb, me, z, screen, whole, zsend, zrecv)
    points = Line(n_orb, me, z, coeffs, rows, csend, crecv)
    tiles.start()

    def direct(mask):
        return remote(coeffs, panel.at[me], psend.at[mask // 2], precv.at[mask // 2], flip(me, mask), z)

    for mask in masks:
        direct(mask).start()

    def forward(mask):
        owner = flip(me, mask)
        block = coeffs if mask == 0 else panel.at[owner]
        return remote(block, panel.at[owner], fsend.at[mask // 2], frecv.at[mask // 2], partner, z)

    forward(0).start()
    own_screen = pltpu.make_async_copy(screen, whole.at[z], local.at[0])
    own_coeffs = pltpu.make_async_copy(coeffs, panel.at[me], local.at[1])
    own_points = pltpu.make_async_copy(coeffs, rows.at[z], local.at[2])
    own_screen.start()
    own_coeffs.start()
    own_points.start()
    for distance in range(1, n_orb):
        tiles.step(distance)
    own_screen.wait()
    tiles.sent()
    points.start()

    def fill(peer):
        def one(c, unused):
            slot = slots[peer * cap + c]
            for q in range(n_orb):
                packed[peer, c, :, q * height:(q + 1) * height, :] = whole[q, :, slot]
            return unused

        lax.fori_loop(0, cap, one, 0)

    def deliver(mask):
        peer = flip(me, mask)
        return remote(packed.at[peer], arrived.at[me], xsend.at[mask], xrecv.at[mask], peer, z)

    for mask in order:
        fill(flip(me, mask))
        deliver(mask).start()
    fill(me)
    own_tiles = pltpu.make_async_copy(packed.at[me], arrived.at[me], local.at[3])
    own_tiles.start()

    for mask in masks:
        owner = flip(me, mask)
        remote(coeffs, panel.at[owner], psend.at[mask // 2], precv.at[mask // 2], owner, z).wait_recv()
        forward(mask).start()
    for distance in range(1, n_orb):
        points.step(distance)

    own_coeffs.wait()
    own_points.wait()
    own_tiles.wait()
    for mask in masks:
        direct(mask).wait_send()
    for mask in [0] + masks:
        forward(mask).wait_send()
        owner = flip(partner, mask)
        remote(coeffs, panel.at[owner], fsend.at[mask // 2], frecv.at[mask // 2], partner, z).wait_recv()
    for mask in order:
        deliver(mask).wait_send()
        peer = flip(me, mask)
        remote(packed.at[peer], arrived.at[peer], xsend.at[mask], xrecv.at[mask], peer, z).wait_recv()
    points.sent()


def spread(screen, coeffs, outgoing, n_blk, n_orb):
    dma = pltpu.SemaphoreType.DMA
    times, _, height, width = screen.shape
    cap = outgoing.shape[0] // n_blk
    tiles = (n_blk, cap, times, n_orb * height, width)
    half = n_blk // 2
    return pl.pallas_call(
        functools.partial(spread_kernel, n_blk, n_orb, cap),
        out_shape=(
            jax.ShapeDtypeStruct(tiles, screen.dtype),
            jax.ShapeDtypeStruct((n_blk,) + coeffs.shape, coeffs.dtype),
            jax.ShapeDtypeStruct((n_orb,) + coeffs.shape, coeffs.dtype),
        ),
        in_specs=[pl.BlockSpec(memory_space=pltpu.SMEM), ANY, ANY],
        out_specs=(ANY, ANY, ANY),
        scratch_shapes=[
            pltpu.VMEM((n_orb,) + screen.shape, screen.dtype),
            pltpu.VMEM(tiles, screen.dtype),
            dma((4,)), dma((2, n_orb)), dma((n_orb,)), dma((2, n_orb)), dma((n_orb,)),
            dma((half,)), dma((half,)), dma((half,)), dma((half,)), dma((n_blk,)), dma((n_blk,)),
        ],
        compiler_params=pltpu.CompilerParams(
            collective_id=1, has_side_effects=True, vmem_limit_bytes=56 * 2**20
        ),
        name="spread",
    )(outgoing, screen, coeffs)


def rows_kernel(count, codes, targets, columns, green, screen, block, out, acc):
    slot = pl.program_id(0)
    orbitals = block.shape[2]

    @pl.when(slot == 0)
    def _():
        acc[...] = jnp.zeros_like(acc)

    @pl.when(slot < count[0])
    def _():
        target = targets[slot]
        for t in range(green.shape[0]):
            sigma = (-(green[t, 0].astype(jnp.float32) * screen[0, t].astype(jnp.float32))).astype(jnp.bfloat16)
            acc[target, :, t * orbitals:(t + 1) * orbitals] += jnp.dot(
                sigma, block[0], preferred_element_type=jnp.float32
            )

    @pl.when(slot == pl.num_programs(0) - 1)
    def _():
        for i in range(acc.shape[0]):
            out[i] = acc[i].astype(out.dtype)


def row_sums(green, arrived, blocks, count, codes, targets, columns, owned):
    times, slots, width, _ = green.shape
    orbitals = blocks.shape[2]

    def live(s, count):
        return jnp.minimum(s, count[0] - 1)

    return pl.pallas_call(
        rows_kernel,
        out_shape=jax.ShapeDtypeStruct((owned, width, times * orbitals), jnp.bfloat16),
        grid_spec=pltpu.PrefetchScalarGridSpec(
            num_scalar_prefetch=4,
            grid=(slots,),
            in_specs=[
                pl.BlockSpec((times, 1, width, width), lambda s, n, c, r, k: (0, live(s, n), 0, 0)),
                pl.BlockSpec((1, times, width, width), lambda s, n, c, r, k: (c[live(s, n)], 0, 0, 0)),
                pl.BlockSpec((1, width, orbitals), lambda s, n, c, r, k: (k[live(s, n)], 0, 0)),
            ],
            out_specs=pl.BlockSpec((owned, width, times * orbitals), lambda s, n, c, r, k: (0, 0, 0)),
            scratch_shapes=[pltpu.VMEM((owned, width, times * orbitals), jnp.float32)],
        ),
        compiler_params=pltpu.CompilerParams(vmem_limit_bytes=56 * 2**20),
        name="row_sums",
    )(count, codes, targets, columns, green, arrived, blocks)


def scatter_kernel(n_blk, part, out, first, second, stage, total, ssend, srecv, send, recv):
    me, z = lax.axis_index("blk"), lax.axis_index("orb")
    partner = flip(me, 1)
    masks = sorted(range(2, n_blk, 2), key=lambda mask: -bin(mask).count("1"))
    barrier = pltpu.get_barrier_semaphore()
    for mask in [1] + masks:
        greet(barrier, flip(me, mask), z)
    pl.semaphore_wait(barrier, len(masks) + 1)

    def to_partner(mask):
        h = mask // 2
        return remote(part.at[flip(partner, mask)], first.at[h], ssend.at[h], srecv.at[h], partner, z)

    def to_owner(mask):
        h = mask // 2
        return remote(stage.at[h], second.at[h], send.at[h], recv.at[h], flip(me, mask), z)

    for mask in masks + [0]:
        to_partner(mask).start()
    for mask in masks:
        h = mask // 2
        to_partner(mask).wait_recv()
        stage[h] = (part[flip(me, mask)].astype(jnp.float32) + first[h].astype(jnp.float32)).astype(stage.dtype)
        to_owner(mask).start()
    to_partner(0).wait_recv()
    total[...] = part[me].astype(jnp.float32) + first[0].astype(jnp.float32)
    for mask in masks[::-1]:
        to_owner(mask).wait_recv()
        total[...] += second[mask // 2].astype(jnp.float32)
    out[...] = total[...]
    for mask in masks + [0]:
        to_partner(mask).wait_send()
    for mask in masks:
        to_owner(mask).wait_send()


def scatter(part):
    n_blk, rows, columns = part.shape
    half = n_blk // 2
    dma = pltpu.SemaphoreType.DMA
    vmem = pl.BlockSpec(memory_space=pltpu.VMEM)
    return pl.pallas_call(
        functools.partial(scatter_kernel, n_blk),
        out_shape=jax.ShapeDtypeStruct((rows, columns), jnp.float32),
        in_specs=[vmem],
        out_specs=vmem,
        scratch_shapes=[
            pltpu.VMEM((half, rows, columns), jnp.bfloat16),
            pltpu.VMEM((half, rows, columns), jnp.bfloat16),
            pltpu.VMEM((half, rows, columns), jnp.bfloat16),
            pltpu.VMEM((rows, columns), jnp.float32),
            dma((half,)), dma((half,)), dma((half,)), dma((half,)),
        ],
        compiler_params=pltpu.CompilerParams(
            collective_id=3, has_side_effects=True, vmem_limit_bytes=32 * 2**20
        ),
        name="scatter",
    )(part)


def shards(
    n_blk, n_orb, green_tiles, screen_tiles, coeffs, tile_count, send_slot, recv_index, row_block, col_block
):
    times, _, width, _ = green_tiles.shape
    owned = coeffs.shape[0] // width
    orbitals = coeffs.shape[1]
    arrived, panel, own_rows = spread(screen_tiles, coeffs, send_slot.reshape(-1), n_blk, n_orb)
    folded = row_sums(
        green_tiles, arrived.reshape((-1,) + arrived.shape[2:]), panel.reshape(-1, width, orbitals),
        tile_count, recv_index[0], row_block[0], col_block[0], owned,
    ).reshape(owned * width, times * orbitals)
    part = jnp.einsum("zkn,km->znm", own_rows, folded, preferred_element_type=jnp.float32)
    part = part.astype(jnp.bfloat16).reshape(n_blk, -1, times * orbitals)
    return scatter(part).reshape(-1, times, orbitals)


def solution(mesh):
    return jax.shard_map(
        functools.partial(shards, mesh.shape["blk"], mesh.shape["orb"]),
        mesh=mesh,
        in_specs=(
            P(None, "blk", None, None),
            P(None, "blk", "orb", None),
            P("blk", "orb"),
            P("blk"),
            P("blk", None, None),
            P("blk", None),
            P("blk", None),
            P("blk", None),
        ),
        out_specs=P("blk", None, "orb"),
        check_vma=False,
    )
```

```python
import functools

import jax
import jax.numpy as jnp
from jax import lax
from jax.experimental import pallas as pl
from jax.experimental.pallas import tpu as pltpu
from jax.sharding import PartitionSpec as P

MESH = pl.DeviceIdType.MESH
ANY = pl.BlockSpec(memory_space=pl.ANY)


def flip(index, mask):
    bit = 1
    while bit <= mask:
        if mask & bit:
            index = index + bit * (1 - 2 * lax.rem(lax.div(index, bit), 2))
        bit *= 2
    return index


def remote(src, dst, send, recv, blk, orb):
    return pltpu.make_async_remote_copy(
        src_ref=src, dst_ref=dst, send_sem=send, recv_sem=recv,
        device_id=(blk, orb), device_id_type=MESH,
    )


def greet(barrier, blk, orb):
    pl.semaphore_signal(barrier, inc=1, device_id=(blk, orb), device_id_type=MESH)


def line_peers(z, n_orb):
    return jnp.minimum(z, 1) + jnp.minimum(n_orb - 1 - z, 1)


class Line:
    def __init__(self, n_orb, me, z, own, held, send, recv):
        self.n_orb, self.me, self.z, self.own = n_orb, me, z, own
        self.held, self.send, self.recv = held, send, recv

    def down(self, src, block=None):
        block = self.held.at[src] if block is None else block
        return remote(block, self.held.at[src], self.send.at[0, src], self.recv.at[src], self.me, self.z - 1)

    def up(self, src, block=None):
        block = self.held.at[src] if block is None else block
        return remote(block, self.held.at[src], self.send.at[1, src], self.recv.at[src], self.me, self.z + 1)

    def start(self):
        @pl.when(self.z > 0)
        def _():
            self.down(self.z, self.own).start()

        @pl.when(self.z < self.n_orb - 1)
        def _():
            self.up(self.z, self.own).start()

    def step(self, distance):
        @pl.when(self.z - distance >= 0)
        def _():
            src = self.z - distance
            self.up(src).wait_recv()

            @pl.when(self.z < self.n_orb - 1)
            def _():
                self.up(src).start()

        @pl.when(self.z + distance < self.n_orb)
        def _():
            src = self.z + distance
            self.down(src).wait_recv()

            @pl.when(self.z > 0)
            def _():
                self.down(src).start()

    def sent(self):
        for src in range(self.n_orb):
            @pl.when((self.z > 0) & (src >= self.z))
            def _():
                self.down(src).wait_send()

            @pl.when((self.z < self.n_orb - 1) & (src <= self.z))
            def _():
                self.up(src).wait_send()


def spread_kernel(n_blk, n_orb, cap, slots, screen, coeffs, arrived, panel, rows, whole, packed, local, zsend,
                  zrecv, csend, crecv, psend, precv, fsend, frecv, xsend, xrecv, rsend, rrecv):
    me, z = lax.axis_index("blk"), lax.axis_index("orb")
    partner = flip(me, 1)
    masks = list(range(2, n_blk, 2))
    relayed = [mask for mask in masks if bin(mask).count("1") == 2]
    plain = [mask for mask in masks if mask not in relayed]
    part = coeffs.shape[0] // 2
    order = sorted(range(1, n_blk), key=lambda mask: -bin(mask).count("1"))
    height = screen.shape[2]
    barrier = pltpu.get_barrier_semaphore()

    @pl.when(z > 0)
    def _():
        greet(barrier, me, z - 1)

    @pl.when(z < n_orb - 1)
    def _():
        greet(barrier, me, z + 1)

    for mask in range(1, n_blk):
        greet(barrier, flip(me, mask), z)
    pl.semaphore_wait(barrier, n_blk - 1 + line_peers(z, n_orb))

    tiles = Line(n_orb, me, z, screen, whole, zsend, zrecv)
    points = Line(n_orb, me, z, coeffs, rows, csend, crecv)
    tiles.start()

    def direct(mask):
        return remote(coeffs, panel.at[me], psend.at[mask // 2], precv.at[mask // 2], flip(me, mask), z)

    for mask in plain:
        direct(mask).start()

    def relay(mask, i):
        low = mask & -mask
        via = (low, mask - low)[i]
        block = panel.at[flip(me, mask - via), pl.ds(i * part, part)]
        return remote(block, block, rsend.at[i, mask // 2], rrecv.at[i, mask // 2], flip(me, via), z)

    def relay_arrives(mask, i):
        block = panel.at[flip(me, mask), pl.ds(i * part, part)]
        remote(block, block, rsend.at[i, mask // 2], rrecv.at[i, mask // 2], partner, z).wait_recv()

    def forward(mask):
        owner = flip(me, mask)
        block = coeffs if mask == 0 else panel.at[owner]
        return remote(block, panel.at[owner], fsend.at[mask // 2], frecv.at[mask // 2], partner, z)

    forward(0).start()
    own_screen = pltpu.make_async_copy(screen, whole.at[z], local.at[0])
    own_coeffs = pltpu.make_async_copy(coeffs, panel.at[me], local.at[1])
    own_points = pltpu.make_async_copy(coeffs, rows.at[z], local.at[2])
    own_screen.start()
    own_coeffs.start()
    own_points.start()
    for distance in range(1, n_orb):
        if distance == n_orb - 1:
            for mask in plain:
                owner = flip(me, mask)
                remote(coeffs, panel.at[owner], psend.at[mask // 2], precv.at[mask // 2], owner, z).wait_recv()
            for mask in relayed:
                relay(mask, 0).start()
                relay(mask, 1).start()
            for mask in plain:
                forward(mask).start()
        tiles.step(distance)
    own_screen.wait()
    tiles.sent()
    points.start()

    def fill(peer):
        def one(c, unused):
            slot = slots[peer * cap + c]
            for q in range(n_orb):
                packed[peer, c, :, q * height:(q + 1) * height, :] = whole[q, :, slot]
            return unused

        lax.fori_loop(0, cap, one, 0)

    def deliver(mask):
        peer = flip(me, mask)
        return remote(packed.at[peer], arrived.at[me], xsend.at[mask], xrecv.at[mask], peer, z)

    for mask in order:
        fill(flip(me, mask))
        deliver(mask).start()
    fill(me)
    own_tiles = pltpu.make_async_copy(packed.at[me], arrived.at[me], local.at[3])
    own_tiles.start()

    for mask in relayed:
        relay_arrives(mask, 0)
        relay_arrives(mask, 1)
        forward(mask).start()
    for distance in range(1, n_orb):
        points.step(distance)

    own_coeffs.wait()
    own_points.wait()
    own_tiles.wait()
    for mask in plain:
        direct(mask).wait_send()
    for mask in relayed:
        relay(mask, 0).wait_send()
        relay(mask, 1).wait_send()
    for mask in [0] + masks:
        forward(mask).wait_send()
        owner = flip(partner, mask)
        remote(coeffs, panel.at[owner], fsend.at[mask // 2], frecv.at[mask // 2], partner, z).wait_recv()
    for mask in order:
        deliver(mask).wait_send()
        peer = flip(me, mask)
        remote(packed.at[peer], arrived.at[peer], xsend.at[mask], xrecv.at[mask], peer, z).wait_recv()
    points.sent()


def spread(screen, coeffs, outgoing, n_blk, n_orb):
    dma = pltpu.SemaphoreType.DMA
    times, _, height, width = screen.shape
    cap = outgoing.shape[0] // n_blk
    tiles = (n_blk, cap, times, n_orb * height, width)
    half = n_blk // 2
    return pl.pallas_call(
        functools.partial(spread_kernel, n_blk, n_orb, cap),
        out_shape=(
            jax.ShapeDtypeStruct(tiles, screen.dtype),
            jax.ShapeDtypeStruct((n_blk,) + coeffs.shape, coeffs.dtype),
            jax.ShapeDtypeStruct((n_orb,) + coeffs.shape, coeffs.dtype),
        ),
        in_specs=[pl.BlockSpec(memory_space=pltpu.SMEM), ANY, ANY],
        out_specs=(ANY, ANY, ANY),
        scratch_shapes=[
            pltpu.VMEM((n_orb,) + screen.shape, screen.dtype),
            pltpu.VMEM(tiles, screen.dtype),
            dma((4,)), dma((2, n_orb)), dma((n_orb,)), dma((2, n_orb)), dma((n_orb,)),
            dma((half,)), dma((half,)), dma((half,)), dma((half,)), dma((n_blk,)), dma((n_blk,)),
            dma((2, half)), dma((2, half)),
        ],
        compiler_params=pltpu.CompilerParams(
            collective_id=1, has_side_effects=True, vmem_limit_bytes=56 * 2**20
        ),
        name="spread",
    )(outgoing, screen, coeffs)


GROUP = 4


def rows_kernel(count, codes, targets, columns, *refs):
    step = pl.program_id(0)
    greens, screens, blocks = (refs[i * GROUP:(i + 1) * GROUP] for i in range(3))
    out, acc = refs[3 * GROUP:]
    orbitals = blocks[0].shape[2]

    @pl.when(step == 0)
    def _():
        acc[...] = jnp.zeros_like(acc)

    for g in range(GROUP):
        slot = step * GROUP + g

        @pl.when(slot < count[0])
        def _():
            target = targets[slot]
            for t in range(greens[g].shape[0]):
                sigma = -(greens[g][t, 0].astype(jnp.float32) * screens[g][0, t].astype(jnp.float32))
                acc[target, :, t * orbitals:(t + 1) * orbitals] += jnp.dot(
                    sigma.astype(jnp.bfloat16), blocks[g][0], preferred_element_type=jnp.float32
                )

    @pl.when(step == pl.num_programs(0) - 1)
    def _():
        for i in range(acc.shape[0]):
            out[i] = acc[i].astype(out.dtype)


def row_sums(green, arrived, blocks, count, codes, targets, columns, owned):
    times, slots, width, _ = green.shape
    orbitals = blocks.shape[2]

    def live(s, g, count):
        return jnp.minimum(s * GROUP + g, count[0] - 1)

    def green_spec(g):
        return pl.BlockSpec((times, 1, width, width), lambda s, n, c, r, k: (0, live(s, g, n), 0, 0))

    def screen_spec(g):
        return pl.BlockSpec((1, times, width, width), lambda s, n, c, r, k: (c[live(s, g, n)], 0, 0, 0))

    def block_spec(g):
        return pl.BlockSpec((1, width, orbitals), lambda s, n, c, r, k: (k[live(s, g, n)], 0, 0))

    specs = [spec(g) for spec in (green_spec, screen_spec, block_spec) for g in range(GROUP)]
    return pl.pallas_call(
        rows_kernel,
        out_shape=jax.ShapeDtypeStruct((owned, width, times * orbitals), jnp.bfloat16),
        grid_spec=pltpu.PrefetchScalarGridSpec(
            num_scalar_prefetch=4,
            grid=(slots // GROUP,),
            in_specs=specs,
            out_specs=pl.BlockSpec((owned, width, times * orbitals), lambda s, n, c, r, k: (0, 0, 0)),
            scratch_shapes=[pltpu.VMEM((owned, width, times * orbitals), jnp.float32)],
        ),
        compiler_params=pltpu.CompilerParams(vmem_limit_bytes=56 * 2**20),
        name="row_sums",
    )(count, codes, targets, columns, *([green] * GROUP + [arrived] * GROUP + [blocks] * GROUP))


def scatter_kernel(n_blk, points, sums, out, mine, leaving, first, second, stage, ssend, srecv, send, recv):
    me, z = lax.axis_index("blk"), lax.axis_index("orb")
    partner = flip(me, 1)
    masks = sorted(range(2, n_blk, 2), key=lambda mask: -bin(mask).count("1"))
    rows = out.shape[0]
    per = points.shape[2] // rows
    barrier = pltpu.get_barrier_semaphore()
    for mask in [1] + masks:
        greet(barrier, flip(me, mask), z)
    pl.semaphore_wait(barrier, len(masks) + 1)

    def chunk(owner):
        start = pl.multiple_of(lax.rem(owner, per) * rows, rows)
        return lax.dot_general(
            points[lax.div(owner, per), :, pl.ds(start, rows)], sums[...], (((0,), (0,)), ((), ())),
            preferred_element_type=jnp.float32,
        )

    def to_partner(mask):
        h = mask // 2
        return remote(leaving.at[h], first.at[h], ssend.at[h], srecv.at[h], partner, z)

    def to_owner(mask):
        h = mask // 2
        return remote(stage.at[h], second.at[h], send.at[h], recv.at[h], flip(me, mask), z)

    def finish(mask):
        h = mask // 2
        to_partner(mask).wait_recv()
        if mask:
            stage[h] = (mine[h] + first[h].astype(jnp.float32)).astype(stage.dtype)
            to_owner(mask).start()
        else:
            out[...] = mine[h] + first[h].astype(jnp.float32)

    turns = masks + [0]
    for i, mask in enumerate(turns):
        h = mask // 2
        leaving[h] = chunk(flip(partner, mask)).astype(leaving.dtype)
        to_partner(mask).start()
        mine[h] = chunk(flip(me, mask))
        if i:
            finish(turns[i - 1])
    finish(0)
    for mask in masks[::-1]:
        to_owner(mask).wait_recv()
        out[...] += second[mask // 2].astype(jnp.float32)
    for mask in turns:
        to_partner(mask).wait_send()
    for mask in masks:
        to_owner(mask).wait_send()


def scatter(points, sums, n_blk):
    rows, columns = points.shape[0] * points.shape[2] // n_blk, sums.shape[1]
    half = n_blk // 2
    dma = pltpu.SemaphoreType.DMA
    vmem = pl.BlockSpec(memory_space=pltpu.VMEM)
    chunks = pltpu.VMEM((half, rows, columns), jnp.bfloat16)
    return pl.pallas_call(
        functools.partial(scatter_kernel, n_blk),
        out_shape=jax.ShapeDtypeStruct((rows, columns), jnp.float32),
        in_specs=[vmem, vmem],
        out_specs=vmem,
        scratch_shapes=[
            pltpu.VMEM((half, rows, columns), jnp.float32), chunks, chunks, chunks, chunks,
            dma((half,)), dma((half,)), dma((half,)), dma((half,)),
        ],
        compiler_params=pltpu.CompilerParams(
            collective_id=3, has_side_effects=True, vmem_limit_bytes=48 * 2**20
        ),
        name="scatter",
    )(points, sums)


def shards(
    n_blk, n_orb, green_tiles, screen_tiles, coeffs, tile_count, send_slot, recv_index, row_block, col_block
):
    times, _, width, _ = green_tiles.shape
    owned = coeffs.shape[0] // width
    orbitals = coeffs.shape[1]
    arrived, panel, own_rows = spread(screen_tiles, coeffs, send_slot.reshape(-1), n_blk, n_orb)
    folded = row_sums(
        green_tiles, arrived.reshape((-1,) + arrived.shape[2:]), panel.reshape(-1, width, orbitals),
        tile_count, recv_index[0], row_block[0], col_block[0], owned,
    ).reshape(owned * width, times * orbitals)
    return scatter(own_rows, folded, n_blk).reshape(-1, times, orbitals)


def solution(mesh):
    return jax.shard_map(
        functools.partial(shards, mesh.shape["blk"], mesh.shape["orb"]),
        mesh=mesh,
        in_specs=(
            P(None, "blk", None, None),
            P(None, "blk", "orb", None),
            P("blk", "orb"),
            P("blk"),
            P("blk", None, None),
            P("blk", None),
            P("blk", None),
            P("blk", None),
        ),
        out_specs=P("blk", None, "orb"),
        check_vma=False,
    )
```

```python
import functools

import jax
import jax.numpy as jnp
from jax import lax
from jax.experimental import pallas as pl
from jax.experimental.pallas import tpu as pltpu
from jax.sharding import PartitionSpec as P

MESH = pl.DeviceIdType.MESH
ANY = pl.BlockSpec(memory_space=pl.ANY)


def flip(index, mask):
    bit = 1
    while bit <= mask:
        if mask & bit:
            index = index + bit * (1 - 2 * lax.rem(lax.div(index, bit), 2))
        bit *= 2
    return index


def remote(src, dst, send, recv, blk, orb):
    return pltpu.make_async_remote_copy(
        src_ref=src, dst_ref=dst, send_sem=send, recv_sem=recv,
        device_id=(blk, orb), device_id_type=MESH,
    )


def greet(barrier, blk, orb):
    pl.semaphore_signal(barrier, inc=1, device_id=(blk, orb), device_id_type=MESH)


def line_peers(z, n_orb):
    return jnp.minimum(z, 1) + jnp.minimum(n_orb - 1 - z, 1)


class Line:
    def __init__(self, n_orb, me, z, own, held, send, recv):
        self.n_orb, self.me, self.z, self.own = n_orb, me, z, own
        self.held, self.send, self.recv = held, send, recv

    def down(self, src, block=None):
        block = self.held.at[src] if block is None else block
        return remote(block, self.held.at[src], self.send.at[0, src], self.recv.at[src], self.me, self.z - 1)

    def up(self, src, block=None):
        block = self.held.at[src] if block is None else block
        return remote(block, self.held.at[src], self.send.at[1, src], self.recv.at[src], self.me, self.z + 1)

    def start(self):
        @pl.when(self.z > 0)
        def _():
            self.down(self.z, self.own).start()

        @pl.when(self.z < self.n_orb - 1)
        def _():
            self.up(self.z, self.own).start()

    def step(self, distance):
        @pl.when(self.z - distance >= 0)
        def _():
            src = self.z - distance
            self.up(src).wait_recv()

            @pl.when(self.z < self.n_orb - 1)
            def _():
                self.up(src).start()

        @pl.when(self.z + distance < self.n_orb)
        def _():
            src = self.z + distance
            self.down(src).wait_recv()

            @pl.when(self.z > 0)
            def _():
                self.down(src).start()

    def then(self, turn, following):
        @pl.when((self.z == turn) & (self.z < self.n_orb - 1))
        def _():
            for src in range(turn + 1):
                self.up(src).wait_send()
            following.up(self.z, following.own).start()

        @pl.when((self.z == self.n_orb - 1 - turn) & (self.z > 0))
        def _():
            for src in range(self.n_orb - 1 - turn, self.n_orb):
                self.down(src).wait_send()
            following.down(self.z, following.own).start()

    def sent(self):
        for src in range(self.n_orb):
            @pl.when((self.z > 0) & (src >= self.z))
            def _():
                self.down(src).wait_send()

            @pl.when((self.z < self.n_orb - 1) & (src <= self.z))
            def _():
                self.up(src).wait_send()


def spread_kernel(n_blk, n_orb, cap, slots, screen, coeffs, arrived, panel, rows, whole, packed, local, zsend,
                  zrecv, csend, crecv, psend, precv, fsend, frecv, xsend, xrecv, rsend, rrecv):
    me, z = lax.axis_index("blk"), lax.axis_index("orb")
    partner = flip(me, 1)
    masks = list(range(2, n_blk, 2))
    relayed = [mask for mask in masks if bin(mask).count("1") == 2]
    plain = [mask for mask in masks if mask not in relayed]
    part = coeffs.shape[0] // 2
    order = sorted(range(1, n_blk), key=lambda mask: -bin(mask).count("1"))
    height = screen.shape[2]
    barrier = pltpu.get_barrier_semaphore()

    @pl.when(z > 0)
    def _():
        greet(barrier, me, z - 1)

    @pl.when(z < n_orb - 1)
    def _():
        greet(barrier, me, z + 1)

    for mask in range(1, n_blk):
        greet(barrier, flip(me, mask), z)
    pl.semaphore_wait(barrier, n_blk - 1 + line_peers(z, n_orb))

    tiles = Line(n_orb, me, z, screen, whole, zsend, zrecv)
    points = Line(n_orb, me, z, coeffs, rows, csend, crecv)
    tiles.start()

    def direct(mask):
        return remote(coeffs, panel.at[me], psend.at[mask // 2], precv.at[mask // 2], flip(me, mask), z)

    for mask in plain:
        direct(mask).start()

    def relay(mask, i):
        low = mask & -mask
        via = (low, mask - low)[i]
        block = panel.at[flip(me, mask - via), pl.ds(i * part, part)]
        return remote(block, block, rsend.at[i, mask // 2], rrecv.at[i, mask // 2], flip(me, via), z)

    def relay_arrives(mask, i):
        block = panel.at[flip(me, mask), pl.ds(i * part, part)]
        remote(block, block, rsend.at[i, mask // 2], rrecv.at[i, mask // 2], partner, z).wait_recv()

    def forward(mask):
        owner = flip(me, mask)
        block = coeffs if mask == 0 else panel.at[owner]
        return remote(block, panel.at[owner], fsend.at[mask // 2], frecv.at[mask // 2], partner, z)

    forward(0).start()
    own_screen = pltpu.make_async_copy(screen, whole.at[z], local.at[0])
    own_coeffs = pltpu.make_async_copy(coeffs, panel.at[me], local.at[1])
    own_points = pltpu.make_async_copy(coeffs, rows.at[z], local.at[2])
    own_screen.start()
    own_coeffs.start()
    own_points.start()
    for distance in range(1, n_orb):
        if distance == n_orb - 1:
            for mask in plain:
                owner = flip(me, mask)
                remote(coeffs, panel.at[owner], psend.at[mask // 2], precv.at[mask // 2], owner, z).wait_recv()
            for mask in relayed:
                relay(mask, 0).start()
                relay(mask, 1).start()
            for mask in plain:
                forward(mask).start()
        tiles.then(distance - 1, points)
        tiles.step(distance)
    own_screen.wait()

    def fill(peer):
        def one(c, unused):
            slot = slots[peer * cap + c]
            for q in range(n_orb):
                packed[peer, c, :, q * height:(q + 1) * height, :] = whole[q, :, slot]
            return unused

        lax.fori_loop(0, cap, one, 0)

    def deliver(mask):
        peer = flip(me, mask)
        return remote(packed.at[peer], arrived.at[me], xsend.at[mask], xrecv.at[mask], peer, z)

    for mask in order:
        fill(flip(me, mask))
        deliver(mask).start()
    fill(me)
    own_tiles = pltpu.make_async_copy(packed.at[me], arrived.at[me], local.at[3])
    own_tiles.start()

    for mask in relayed:
        relay_arrives(mask, 0)
        relay_arrives(mask, 1)
        forward(mask).start()
    for distance in range(1, n_orb):
        points.step(distance)

    own_coeffs.wait()
    own_points.wait()
    own_tiles.wait()
    for mask in plain:
        direct(mask).wait_send()
    for mask in relayed:
        relay(mask, 0).wait_send()
        relay(mask, 1).wait_send()
    for mask in [0] + masks:
        forward(mask).wait_send()
        owner = flip(partner, mask)
        remote(coeffs, panel.at[owner], fsend.at[mask // 2], frecv.at[mask // 2], partner, z).wait_recv()
    for mask in order:
        deliver(mask).wait_send()
        peer = flip(me, mask)
        remote(packed.at[peer], arrived.at[peer], xsend.at[mask], xrecv.at[mask], peer, z).wait_recv()
    points.sent()


def spread(screen, coeffs, outgoing, n_blk, n_orb):
    dma = pltpu.SemaphoreType.DMA
    times, _, height, width = screen.shape
    cap = outgoing.shape[0] // n_blk
    tiles = (n_blk, cap, times, n_orb * height, width)
    half = n_blk // 2
    return pl.pallas_call(
        functools.partial(spread_kernel, n_blk, n_orb, cap),
        out_shape=(
            jax.ShapeDtypeStruct(tiles, screen.dtype),
            jax.ShapeDtypeStruct((n_blk,) + coeffs.shape, coeffs.dtype),
            jax.ShapeDtypeStruct((n_orb,) + coeffs.shape, coeffs.dtype),
        ),
        in_specs=[pl.BlockSpec(memory_space=pltpu.SMEM), ANY, ANY],
        out_specs=(ANY, ANY, ANY),
        scratch_shapes=[
            pltpu.VMEM((n_orb,) + screen.shape, screen.dtype),
            pltpu.VMEM(tiles, screen.dtype),
            dma((4,)), dma((2, n_orb)), dma((n_orb,)), dma((2, n_orb)), dma((n_orb,)),
            dma((half,)), dma((half,)), dma((half,)), dma((half,)), dma((n_blk,)), dma((n_blk,)),
            dma((2, half)), dma((2, half)),
        ],
        compiler_params=pltpu.CompilerParams(
            collective_id=1, has_side_effects=True, vmem_limit_bytes=56 * 2**20
        ),
        name="spread",
    )(outgoing, screen, coeffs)


GROUP = 4


def rows_kernel(count, codes, targets, columns, *refs):
    step = pl.program_id(0)
    greens, screens, blocks = (refs[i * GROUP:(i + 1) * GROUP] for i in range(3))
    out, acc = refs[3 * GROUP:]
    orbitals = blocks[0].shape[2]

    @pl.when(step == 0)
    def _():
        acc[...] = jnp.zeros_like(acc)

    for g in range(GROUP):
        slot = step * GROUP + g

        @pl.when(slot < count[0])
        def _():
            target = targets[slot]
            for t in range(greens[g].shape[0]):
                sigma = -(greens[g][t, 0].astype(jnp.float32) * screens[g][0, t].astype(jnp.float32))
                acc[target, :, t * orbitals:(t + 1) * orbitals] += jnp.dot(
                    sigma.astype(jnp.bfloat16), blocks[g][0], preferred_element_type=jnp.float32
                )

    @pl.when(step == pl.num_programs(0) - 1)
    def _():
        for i in range(acc.shape[0]):
            out[i] = acc[i].astype(out.dtype)


def row_sums(green, arrived, blocks, count, codes, targets, columns, owned):
    times, slots, width, _ = green.shape
    orbitals = blocks.shape[2]

    def live(s, g, count):
        return jnp.minimum(s * GROUP + g, count[0] - 1)

    def green_spec(g):
        return pl.BlockSpec((times, 1, width, width), lambda s, n, c, r, k: (0, live(s, g, n), 0, 0))

    def screen_spec(g):
        return pl.BlockSpec((1, times, width, width), lambda s, n, c, r, k: (c[live(s, g, n)], 0, 0, 0))

    def block_spec(g):
        return pl.BlockSpec((1, width, orbitals), lambda s, n, c, r, k: (k[live(s, g, n)], 0, 0))

    specs = [spec(g) for spec in (green_spec, screen_spec, block_spec) for g in range(GROUP)]
    return pl.pallas_call(
        rows_kernel,
        out_shape=jax.ShapeDtypeStruct((owned, width, times * orbitals), jnp.bfloat16),
        grid_spec=pltpu.PrefetchScalarGridSpec(
            num_scalar_prefetch=4,
            grid=(slots // GROUP,),
            in_specs=specs,
            out_specs=pl.BlockSpec((owned, width, times * orbitals), lambda s, n, c, r, k: (0, 0, 0)),
            scratch_shapes=[pltpu.VMEM((owned, width, times * orbitals), jnp.float32)],
        ),
        compiler_params=pltpu.CompilerParams(vmem_limit_bytes=46 * 2**20),
        name="row_sums",
    )(count, codes, targets, columns, *([green] * GROUP + [arrived] * GROUP + [blocks] * GROUP))


def scatter_kernel(n_blk, points, sums, out, mine, leaving, first, second, stage, ssend, srecv, send, recv):
    me, z = lax.axis_index("blk"), lax.axis_index("orb")
    partner = flip(me, 1)
    masks = sorted(range(2, n_blk, 2), key=lambda mask: -bin(mask).count("1"))
    rows = out.shape[0]
    per = points.shape[2] // rows
    barrier = pltpu.get_barrier_semaphore()
    for mask in [1] + masks:
        greet(barrier, flip(me, mask), z)
    pl.semaphore_wait(barrier, len(masks) + 1)

    def chunk(owner):
        start = pl.multiple_of(lax.rem(owner, per) * rows, rows)
        return lax.dot_general(
            points[lax.div(owner, per), :, pl.ds(start, rows)], sums[...], (((0,), (0,)), ((), ())),
            preferred_element_type=jnp.float32,
        )

    def to_partner(mask):
        h = mask // 2
        return remote(leaving.at[h], first.at[h], ssend.at[h], srecv.at[h], partner, z)

    def to_owner(mask):
        h = mask // 2
        return remote(stage.at[h], second.at[h], send.at[h], recv.at[h], flip(me, mask), z)

    def finish(mask):
        h = mask // 2
        to_partner(mask).wait_recv()
        if mask:
            stage[h] = (mine[h] + first[h].astype(jnp.float32)).astype(stage.dtype)
            to_owner(mask).start()
        else:
            out[...] = mine[h] + first[h].astype(jnp.float32)

    turns = masks + [0]
    for i, mask in enumerate(turns):
        h = mask // 2
        leaving[h] = chunk(flip(partner, mask)).astype(leaving.dtype)
        to_partner(mask).start()
        mine[h] = chunk(flip(me, mask))
        if i:
            finish(turns[i - 1])
    finish(0)
    for mask in masks[::-1]:
        to_owner(mask).wait_recv()
        out[...] += second[mask // 2].astype(jnp.float32)
    for mask in turns:
        to_partner(mask).wait_send()
    for mask in masks:
        to_owner(mask).wait_send()


def scatter(points, sums, n_blk):
    rows, columns = points.shape[0] * points.shape[2] // n_blk, sums.shape[1]
    half = n_blk // 2
    dma = pltpu.SemaphoreType.DMA
    vmem = pl.BlockSpec(memory_space=pltpu.VMEM)
    chunks = pltpu.VMEM((half, rows, columns), jnp.bfloat16)
    return pl.pallas_call(
        functools.partial(scatter_kernel, n_blk),
        out_shape=jax.ShapeDtypeStruct((rows, columns), jnp.float32),
        in_specs=[vmem, vmem],
        out_specs=vmem,
        scratch_shapes=[
            pltpu.VMEM((half, rows, columns), jnp.float32), chunks, chunks, chunks, chunks,
            dma((half,)), dma((half,)), dma((half,)), dma((half,)),
        ],
        compiler_params=pltpu.CompilerParams(
            collective_id=3, has_side_effects=True, vmem_limit_bytes=48 * 2**20
        ),
        name="scatter",
    )(points, sums)


def shards(
    n_blk, n_orb, green_tiles, screen_tiles, coeffs, tile_count, send_slot, recv_index, row_block, col_block
):
    times, _, width, _ = green_tiles.shape
    owned = coeffs.shape[0] // width
    orbitals = coeffs.shape[1]
    arrived, panel, own_rows = spread(screen_tiles, coeffs, send_slot.reshape(-1), n_blk, n_orb)
    folded = row_sums(
        green_tiles, arrived.reshape((-1,) + arrived.shape[2:]), panel.reshape(-1, width, orbitals),
        tile_count, recv_index[0], row_block[0], col_block[0], owned,
    ).reshape(owned * width, times * orbitals)
    return scatter(own_rows, folded, n_blk).reshape(-1, times, orbitals)


def solution(mesh):
    return jax.shard_map(
        functools.partial(shards, mesh.shape["blk"], mesh.shape["orb"]),
        mesh=mesh,
        in_specs=(
            P(None, "blk", None, None),
            P(None, "blk", "orb", None),
            P("blk", "orb"),
            P("blk"),
            P("blk", None, None),
            P("blk", None),
            P("blk", None),
            P("blk", None),
        ),
        out_specs=P("blk", None, "orb"),
        check_vma=False,
    )
```

```python
import functools

import jax
import jax.numpy as jnp
from jax import lax
from jax.experimental import pallas as pl
from jax.experimental.pallas import tpu as pltpu
from jax.sharding import PartitionSpec as P

MESH = pl.DeviceIdType.MESH
ANY = pl.BlockSpec(memory_space=pl.ANY)


def flip(index, mask):
    bit = 1
    while bit <= mask:
        if mask & bit:
            index = index + bit * (1 - 2 * lax.rem(lax.div(index, bit), 2))
        bit *= 2
    return index


def remote(src, dst, send, recv, blk, orb):
    return pltpu.make_async_remote_copy(
        src_ref=src, dst_ref=dst, send_sem=send, recv_sem=recv,
        device_id=(blk, orb), device_id_type=MESH,
    )


def greet(barrier, blk, orb):
    pl.semaphore_signal(barrier, inc=1, device_id=(blk, orb), device_id_type=MESH)


def line_peers(z, n_orb):
    return jnp.minimum(z, 1) + jnp.minimum(n_orb - 1 - z, 1)


class Line:
    def __init__(self, n_orb, me, z, own, held, send, recv):
        self.n_orb, self.me, self.z, self.own = n_orb, me, z, own
        self.held, self.send, self.recv = held, send, recv

    def down(self, src, block=None):
        block = self.held.at[src] if block is None else block
        return remote(block, self.held.at[src], self.send.at[0, src], self.recv.at[src], self.me, self.z - 1)

    def up(self, src, block=None):
        block = self.held.at[src] if block is None else block
        return remote(block, self.held.at[src], self.send.at[1, src], self.recv.at[src], self.me, self.z + 1)

    def start(self):
        @pl.when(self.z > 0)
        def _():
            self.down(self.z, self.own).start()

        @pl.when(self.z < self.n_orb - 1)
        def _():
            self.up(self.z, self.own).start()

    def step(self, distance):
        @pl.when(self.z - distance >= 0)
        def _():
            src = self.z - distance
            self.up(src).wait_recv()

            @pl.when(self.z < self.n_orb - 1)
            def _():
                self.up(src).start()

        @pl.when(self.z + distance < self.n_orb)
        def _():
            src = self.z + distance
            self.down(src).wait_recv()

            @pl.when(self.z > 0)
            def _():
                self.down(src).start()

    def then(self, turn, following):
        @pl.when((self.z == turn) & (self.z < self.n_orb - 1))
        def _():
            for src in range(turn + 1):
                self.up(src).wait_send()
            following.up(self.z, following.own).start()

        @pl.when((self.z == self.n_orb - 1 - turn) & (self.z > 0))
        def _():
            for src in range(self.n_orb - 1 - turn, self.n_orb):
                self.down(src).wait_send()
            following.down(self.z, following.own).start()

    def sent(self):
        for src in range(self.n_orb):
            @pl.when((self.z > 0) & (src >= self.z))
            def _():
                self.down(src).wait_send()

            @pl.when((self.z < self.n_orb - 1) & (src <= self.z))
            def _():
                self.up(src).wait_send()


def spread_kernel(n_blk, n_orb, cap, slots, screen, coeffs, arrived, panel, rows, whole, packed, local, zsend,
                  zrecv, csend, crecv, psend, precv, fsend, frecv, xsend, xrecv, rsend, rrecv):
    me, z = lax.axis_index("blk"), lax.axis_index("orb")
    partner = flip(me, 1)
    masks = list(range(2, n_blk, 2))
    relayed = [mask for mask in masks if bin(mask).count("1") == 2]
    plain = [mask for mask in masks if mask not in relayed]
    part = coeffs.shape[0] // 2
    order = sorted(range(1, n_blk), key=lambda mask: -bin(mask).count("1"))
    height = screen.shape[2]
    barrier = pltpu.get_barrier_semaphore()

    @pl.when(z > 0)
    def _():
        greet(barrier, me, z - 1)

    @pl.when(z < n_orb - 1)
    def _():
        greet(barrier, me, z + 1)

    for mask in range(1, n_blk):
        greet(barrier, flip(me, mask), z)
    pl.semaphore_wait(barrier, n_blk - 1 + line_peers(z, n_orb))

    tiles = Line(n_orb, me, z, screen, whole, zsend, zrecv)
    points = Line(n_orb, me, z, coeffs, rows, csend, crecv)
    tiles.start()

    def direct(mask):
        return remote(coeffs, panel.at[me], psend.at[mask // 2], precv.at[mask // 2], flip(me, mask), z)

    for mask in plain:
        direct(mask).start()

    def relay(mask, i):
        low = mask & -mask
        via = (low, mask - low)[i]
        block = panel.at[flip(me, mask - via), pl.ds(i * part, part)]
        return remote(block, block, rsend.at[i, mask // 2], rrecv.at[i, mask // 2], flip(me, via), z)

    def relay_arrives(mask, i):
        block = panel.at[flip(me, mask), pl.ds(i * part, part)]
        remote(block, block, rsend.at[i, mask // 2], rrecv.at[i, mask // 2], partner, z).wait_recv()

    def forward(mask):
        owner = flip(me, mask)
        block = coeffs if mask == 0 else panel.at[owner]
        return remote(block, panel.at[owner], fsend.at[mask // 2], frecv.at[mask // 2], partner, z)

    forward(0).start()
    own_screen = pltpu.make_async_copy(screen, whole.at[z], local.at[0])
    own_coeffs = pltpu.make_async_copy(coeffs, panel.at[me], local.at[1])
    own_points = pltpu.make_async_copy(coeffs, rows.at[z], local.at[2])
    own_screen.start()
    own_coeffs.start()
    own_points.start()
    for distance in range(1, n_orb):
        if distance == n_orb - 1:
            for mask in plain:
                owner = flip(me, mask)
                remote(coeffs, panel.at[owner], psend.at[mask // 2], precv.at[mask // 2], owner, z).wait_recv()
            for mask in relayed:
                relay(mask, 0).start()
                relay(mask, 1).start()
            for mask in plain:
                forward(mask).start()
        tiles.then(distance - 1, points)
        tiles.step(distance)
    own_screen.wait()

    def fill(peer):
        def one(c, unused):
            slot = slots[peer * cap + c]
            for q in range(n_orb):
                packed[peer, c, :, q * height:(q + 1) * height, :] = whole[q, :, slot]
            return unused

        lax.fori_loop(0, cap, one, 0)

    def deliver(mask):
        peer = flip(me, mask)
        return remote(packed.at[peer], arrived.at[me], xsend.at[mask], xrecv.at[mask], peer, z)

    for mask in order:
        fill(flip(me, mask))
        deliver(mask).start()
    fill(me)
    own_tiles = pltpu.make_async_copy(packed.at[me], arrived.at[me], local.at[3])
    own_tiles.start()

    for mask in relayed:
        relay_arrives(mask, 0)
        relay_arrives(mask, 1)
        forward(mask).start()
    for distance in range(1, n_orb):
        points.step(distance)

    own_coeffs.wait()
    own_points.wait()
    own_tiles.wait()
    for mask in plain:
        direct(mask).wait_send()
    for mask in relayed:
        relay(mask, 0).wait_send()
        relay(mask, 1).wait_send()
    for mask in [0] + masks:
        forward(mask).wait_send()
        owner = flip(partner, mask)
        remote(coeffs, panel.at[owner], fsend.at[mask // 2], frecv.at[mask // 2], partner, z).wait_recv()
    for mask in order:
        deliver(mask).wait_send()
        peer = flip(me, mask)
        remote(packed.at[peer], arrived.at[peer], xsend.at[mask], xrecv.at[mask], peer, z).wait_recv()
    points.sent()


def spread(screen, coeffs, outgoing, n_blk, n_orb):
    dma = pltpu.SemaphoreType.DMA
    times, _, height, width = screen.shape
    cap = outgoing.shape[0] // n_blk
    tiles = (n_blk, cap, times, n_orb * height, width)
    half = n_blk // 2
    return pl.pallas_call(
        functools.partial(spread_kernel, n_blk, n_orb, cap),
        out_shape=(
            jax.ShapeDtypeStruct(tiles, screen.dtype),
            jax.ShapeDtypeStruct((n_blk,) + coeffs.shape, coeffs.dtype),
            jax.ShapeDtypeStruct((n_orb,) + coeffs.shape, coeffs.dtype),
        ),
        in_specs=[pl.BlockSpec(memory_space=pltpu.SMEM), ANY, ANY],
        out_specs=(ANY, ANY, ANY),
        scratch_shapes=[
            pltpu.VMEM((n_orb,) + screen.shape, screen.dtype),
            pltpu.VMEM(tiles, screen.dtype),
            dma((4,)), dma((2, n_orb)), dma((n_orb,)), dma((2, n_orb)), dma((n_orb,)),
            dma((half,)), dma((half,)), dma((half,)), dma((half,)), dma((n_blk,)), dma((n_blk,)),
            dma((2, half)), dma((2, half)),
        ],
        compiler_params=pltpu.CompilerParams(
            collective_id=1, has_side_effects=True, vmem_limit_bytes=56 * 2**20
        ),
        name="spread",
    )(outgoing, screen, coeffs)


GROUP = 4


def rows_kernel(count, codes, targets, columns, *refs):
    step = pl.program_id(0)
    greens, screens, blocks = (refs[i * GROUP:(i + 1) * GROUP] for i in range(3))
    out, acc = refs[3 * GROUP:]
    orbitals = blocks[0].shape[2]

    @pl.when(step == 0)
    def _():
        acc[...] = jnp.zeros_like(acc)

    for g in range(GROUP):
        slot = step * GROUP + g

        @pl.when(slot < count[0])
        def _():
            target = targets[slot]
            for t in range(greens[g].shape[0]):
                sigma = -(greens[g][t, 0].astype(jnp.float32) * screens[g][0, t].astype(jnp.float32))
                acc[target, :, t * orbitals:(t + 1) * orbitals] += jnp.dot(
                    sigma.astype(jnp.bfloat16), blocks[g][0], preferred_element_type=jnp.float32
                )

    @pl.when(step == pl.num_programs(0) - 1)
    def _():
        for i in range(acc.shape[0]):
            out[i] = acc[i].astype(out.dtype)


def row_sums(green, arrived, blocks, count, codes, targets, columns, owned):
    times, slots, width, _ = green.shape
    orbitals = blocks.shape[2]

    def live(s, g, count):
        return jnp.minimum(s * GROUP + g, count[0] - 1)

    def green_spec(g):
        return pl.BlockSpec((times, 1, width, width), lambda s, n, c, r, k: (0, live(s, g, n), 0, 0))

    def screen_spec(g):
        return pl.BlockSpec((1, times, width, width), lambda s, n, c, r, k: (c[live(s, g, n)], 0, 0, 0))

    def block_spec(g):
        return pl.BlockSpec((1, width, orbitals), lambda s, n, c, r, k: (k[live(s, g, n)], 0, 0))

    specs = [spec(g) for spec in (green_spec, screen_spec, block_spec) for g in range(GROUP)]
    return pl.pallas_call(
        rows_kernel,
        out_shape=jax.ShapeDtypeStruct((owned, width, times * orbitals), jnp.bfloat16),
        grid_spec=pltpu.PrefetchScalarGridSpec(
            num_scalar_prefetch=4,
            grid=(slots // GROUP,),
            in_specs=specs,
            out_specs=pl.BlockSpec((owned, width, times * orbitals), lambda s, n, c, r, k: (0, 0, 0)),
            scratch_shapes=[pltpu.VMEM((owned, width, times * orbitals), jnp.float32)],
        ),
        compiler_params=pltpu.CompilerParams(vmem_limit_bytes=46 * 2**20),
        name="row_sums",
    )(count, codes, targets, columns, *([green] * GROUP + [arrived] * GROUP + [blocks] * GROUP))


def scatter_kernel(n_blk, points, sums, out, mine, leaving, first, second, stage, ssend, srecv, send, recv):
    me, z = lax.axis_index("blk"), lax.axis_index("orb")
    partner = flip(me, 1)
    masks = sorted(range(2, n_blk, 2), key=lambda mask: -bin(mask).count("1"))
    rows = out.shape[0]
    per = points.shape[2] // rows
    barrier = pltpu.get_barrier_semaphore()
    for mask in [1] + masks:
        greet(barrier, flip(me, mask), z)
    pl.semaphore_wait(barrier, len(masks) + 1)

    def chunk(owner):
        start = pl.multiple_of(lax.rem(owner, per) * rows, rows)
        return lax.dot_general(
            points[lax.div(owner, per), :, pl.ds(start, rows)], sums[...], (((0,), (0,)), ((), ())),
            preferred_element_type=jnp.float32,
        )

    def to_partner(mask):
        h = mask // 2
        return remote(leaving.at[h], first.at[h], ssend.at[h], srecv.at[h], partner, z)

    def to_owner(mask):
        h = mask // 2
        return remote(stage.at[h], second.at[h], send.at[h], recv.at[h], flip(me, mask), z)

    def finish(mask):
        h = mask // 2
        to_partner(mask).wait_recv()
        if mask:
            stage[h] = (mine[h] + first[h].astype(jnp.float32)).astype(stage.dtype)
            to_owner(mask).start()
        else:
            out[...] = mine[h] + first[h].astype(jnp.float32)

    turns = masks + [0]

    def leave(mask):
        leaving[mask // 2] = chunk(flip(partner, mask)).astype(leaving.dtype)
        to_partner(mask).start()

    leave(turns[0])
    for i, mask in enumerate(turns):
        mine[mask // 2] = chunk(flip(me, mask))
        if i + 1 < len(turns):
            leave(turns[i + 1])
        finish(mask)
    for mask in masks[::-1]:
        to_owner(mask).wait_recv()
        out[...] += second[mask // 2].astype(jnp.float32)
    for mask in turns:
        to_partner(mask).wait_send()
    for mask in masks:
        to_owner(mask).wait_send()


def scatter(points, sums, n_blk):
    rows, columns = points.shape[0] * points.shape[2] // n_blk, sums.shape[1]
    half = n_blk // 2
    dma = pltpu.SemaphoreType.DMA
    vmem = pl.BlockSpec(memory_space=pltpu.VMEM)
    chunks = pltpu.VMEM((half, rows, columns), jnp.bfloat16)
    return pl.pallas_call(
        functools.partial(scatter_kernel, n_blk),
        out_shape=jax.ShapeDtypeStruct((rows, columns), jnp.float32),
        in_specs=[vmem, vmem],
        out_specs=vmem,
        scratch_shapes=[
            pltpu.VMEM((half, rows, columns), jnp.float32), chunks, chunks, chunks, chunks,
            dma((half,)), dma((half,)), dma((half,)), dma((half,)),
        ],
        compiler_params=pltpu.CompilerParams(
            collective_id=3, has_side_effects=True, vmem_limit_bytes=48 * 2**20
        ),
        name="scatter",
    )(points, sums)


def shards(
    n_blk, n_orb, green_tiles, screen_tiles, coeffs, tile_count, send_slot, recv_index, row_block, col_block
):
    times, _, width, _ = green_tiles.shape
    owned = coeffs.shape[0] // width
    orbitals = coeffs.shape[1]
    arrived, panel, own_rows = spread(screen_tiles, coeffs, send_slot.reshape(-1), n_blk, n_orb)
    folded = row_sums(
        green_tiles, arrived.reshape((-1,) + arrived.shape[2:]), panel.reshape(-1, width, orbitals),
        tile_count, recv_index[0], row_block[0], col_block[0], owned,
    ).reshape(owned * width, times * orbitals)
    return scatter(own_rows, folded, n_blk).reshape(-1, times, orbitals)


def solution(mesh):
    return jax.shard_map(
        functools.partial(shards, mesh.shape["blk"], mesh.shape["orb"]),
        mesh=mesh,
        in_specs=(
            P(None, "blk", None, None),
            P(None, "blk", "orb", None),
            P("blk", "orb"),
            P("blk"),
            P("blk", None, None),
            P("blk", None),
            P("blk", None),
            P("blk", None),
        ),
        out_specs=P("blk", None, "orb"),
        check_vma=False,
    )
```
